128 devices in a mesh: expert: 32 (over y, z, x_hi), shard: 4 (over x_lo, core).
Axes of the slice: x: 4 (x_hi: 2, x_lo: 2; x = x_hi * 2 + x_lo), y: 4, z: 4, core: 2. Of those that a mesh axis runs over, the one named last changes fastest.
Arguments:
- tokens: bfloat16 [512, 4096], P('expert', 'shard'), may hold values from -6 to 6
- routes: int32 [512, 2], P('expert'), may hold values from 0 to 3, all different within a row
- gate_probs: float32 [512, 2], P('expert'), may hold values from 0.1 to 1
- prev_counts: int32 [4], replicated, may hold values from 32 to 192
- hosts: int32 [4], replicated, may hold values from 1 to 6
- w_gate: bfloat16 [32, 4096, 1536], P('expert', None, 'shard'), may hold values from -0.09375 to 0.09375
- w_up: bfloat16 [32, 4096, 1536], P('expert', None, 'shard'), may hold values from -0.09375 to 0.09375
- w_down: bfloat16 [32, 1536, 4096], P('expert', 'shard'), may hold values from -0.0546875 to 0.0546875
- grad_out: bfloat16 [512, 4096], P('expert', 'shard'), may hold values from -6 to 6
Outputs:
- outputs: bfloat16 [512, 4096], P('expert', 'shard')
- grad_tokens: bfloat16 [512, 4096], P('expert', 'shard')
- grad_gate: bfloat16 [32, 4096, 1536], P('expert', None, 'shard')
- grad_up: bfloat16 [32, 4096, 1536], P('expert', None, 'shard')
- grad_down: bfloat16 [32, 1536, 4096], P('expert', 'shard')
The draws below stay inside these ranges and needn't reach their ends.
Inputs may be any that keep to these rules, and one draw needn't show every extreme that they name: `routes`: each token names two different experts.
All inputs are finite; a program needn't handle non-finite values.
Results may differ from the reference program's by a relative error of at most 0.0062.
Values may be sent and summed in bfloat16 or wider, within the bound.
No kernel may reach another device: no remote copies, remote signals or barrier semaphores. Data moves between devices by JAX's collectives and lax.ppermute only.
A program may use at most 192 MiB of HBM per device.

```python
import jax
import jax.numpy as jnp
from jax import lax

D = 4096
FF = 12288
EXPERTS = 4
TOK_RANK = 16
CAP = 6
GROUP = 8
TOKENS = 512
N_EXPERT = 32


def draw_hosts(key, part):
    key = jax.random.fold_in(key, 7)
    first, second = jax.random.split(key)
    values = jax.random.randint(first, (EXPERTS,), 1, CAP + 1, dtype=jnp.int32)
    chosen = jax.random.randint(second, (), 0, EXPERTS, dtype=jnp.int32)
    return jnp.where(jnp.arange(EXPERTS, dtype=jnp.int32) == chosen, CAP, values).astype(jnp.int32)


def with_ends(values, own_key, least, top_value):
    index_at = [jax.random.randint(jax.random.fold_in(own_key, axis), (), 0, length) for axis, length in enumerate(values.shape)]
    main_axis = values.shape.index(max(values.shape))
    next_to = index_at[:main_axis] + [(index_at[main_axis] + 1) % values.shape[main_axis]] + index_at[main_axis + 1:]
    return values.at[tuple(index_at)].set(least).at[tuple(next_to)].set(top_value)


def level_of(rng, dims, pieces, smallest, high):
    gain, own = 1.0, jax.random.fold_in(rng, 6)
    for axis_at, shards_of in pieces:
        heights = jnp.exp(jax.random.uniform(jax.random.fold_in(own, axis_at), (shards_of,), jnp.float32, smallest / len(pieces), high / len(pieces)))
        gain = gain * jnp.repeat(heights, dims[axis_at] // shards_of).reshape([-1 if axis == axis_at else 1 for axis in range(len(dims))])
    return gain


def different_ones(rng, rows, number_of, top, lift):
    ranking = jax.random.permutation(jax.random.fold_in(rng, 1), number_of)
    pull = ranking
    for power in range(3):
        pull = pull * pull // number_of
    pull = pull * lift // number_of
    chance = jax.random.randint(jax.random.fold_in(rng, 2), (rows, number_of), 0, 4096) + pull
    fixed_rows = jax.random.permutation(jax.random.fold_in(rng, 3), rows)[jnp.arange(number_of) % rows]
    chance = jnp.where(jnp.arange(rows)[:, None] == fixed_rows[None, :], 1 << 14, chance)
    priority = chance * number_of + jnp.arange(number_of)
    return lax.top_k(priority.astype(jnp.int32), top)[1].astype(jnp.int32)


def noise(own_key, extent, scale, limit, cuts=(), held_as=jnp.bfloat16):
    drawn = scale * jax.random.normal(own_key, extent, jnp.float32)
    if cuts:
        drawn = drawn * level_of(own_key, extent, cuts, -0.22, 0.18)
    return jnp.clip(drawn, -limit, limit).astype(held_as)


def setup_inputs(seed: int = 0) -> dict:
    arg_keys = jax.random.split(jax.random.key(seed), 10)
    return {
        "tokens": noise(arg_keys[0], (TOKENS, D), 1.0, 6.0, ((0, 32), (1, 4))),
        "routes": different_ones(arg_keys[1], TOKENS, EXPERTS, 2, 8192),
        "gate_probs": jnp.clip(0.1 + 0.9 * jax.random.uniform(arg_keys[2], (TOKENS, 2), jnp.float32) ** level_of(arg_keys[2], (TOKENS, 2), ((0, 32),), -0.2, 0.2), 0.1, 1.0),
        "prev_counts": with_ends(jax.random.randint(arg_keys[3], (EXPERTS,), N_EXPERT, N_EXPERT * CAP + 1), jax.random.fold_in(arg_keys[3], 1), N_EXPERT, N_EXPERT * CAP).astype(jnp.int32),
        "hosts": draw_hosts(jax.random.fold_in(arg_keys[9], 71), 0),
        "w_gate": noise(arg_keys[5], (EXPERTS * GROUP, D, FF // GROUP), D ** -0.5, 0.09375, ((0, 32), (2, 4))),
        "w_up": noise(arg_keys[6], (EXPERTS * GROUP, D, FF // GROUP), D ** -0.5, 0.09375, ((0, 32), (2, 4))),
        "w_down": noise(arg_keys[7], (EXPERTS * GROUP, FF // GROUP, D), FF ** -0.5, 0.0546875, ((0, 32), (1, 4))),
        "grad_out": noise(arg_keys[8], (TOKENS, D), 1.0, 6.0, ((0, 32), (1, 4))),
    }


def silu_parts(gate_vals):
    sigma = jax.nn.sigmoid(gate_vals)
    return gate_vals * sigma, sigma * (1.0 + gate_vals * (1.0 - sigma))


def assign_source(pair_experts, prev_counts, hosts, rank_count):
    count = pair_experts.shape[0]
    expert_ids = jnp.arange(EXPERTS, dtype=jnp.int32)
    partner = hosts.reshape(EXPERTS // 2, 2)[:, ::-1].reshape(EXPERTS)
    divisor = 2 * rank_count
    quota = jnp.minimum((prev_counts + divisor - 1) // divisor, CAP).astype(jnp.int32)
    onehot = pair_experts[:, None] == expert_ids[None, :]
    pair_quota = jnp.sum(jnp.where(onehot, quota[None, :], 0), axis=1, dtype=jnp.int32)
    pair_guest = jnp.sum(jnp.where(onehot, partner[None, :], 0), axis=1, dtype=jnp.int32)
    order_ids = jnp.arange(count, dtype=jnp.int32)
    earlier = order_ids[None, :] < order_ids[:, None]
    same = pair_experts[:, None] == pair_experts[None, :]
    position = jnp.sum(same & earlier, axis=1, dtype=jnp.int32)
    server = (position >= pair_quota).astype(jnp.int32)
    slot_row = position - server * pair_quota
    return server, slot_row, position < pair_quota + pair_guest


def matmul(left, right):
    return jnp.dot(left, right, preferred_element_type=jnp.float32)


def split_sum(home_part, guest_part):
    rounded = lax.optimization_barrier(guest_part.astype(jnp.bfloat16))
    return (home_part + rounded.astype(jnp.float32)).astype(jnp.bfloat16)


def reference(tokens, routes, gate_probs, prev_counts, hosts, w_gate, w_up, w_down, grad_out):
    group_size = N_EXPERT // EXPERTS
    block_width = FF // group_size
    per_source = routes.reshape(N_EXPERT, 2 * TOK_RANK)
    server, slot_row, kept_mask = jax.vmap(lambda source: assign_source(source, prev_counts, hosts, N_EXPERT))(per_source)
    server = server.reshape(TOKENS, 2)
    kept_mask = kept_mask.reshape(TOKENS, 2)
    gate_full = w_gate.reshape(EXPERTS, group_size, D, block_width).transpose(0, 2, 1, 3).reshape(EXPERTS, D, FF)
    up_full = w_up.reshape(EXPERTS, group_size, D, block_width).transpose(0, 2, 1, 3).reshape(EXPERTS, D, FF)
    down_full = w_down.reshape(EXPERTS, FF, D)
    outputs = jnp.zeros((TOKENS, D), jnp.float32)
    grad_tokens = jnp.zeros((TOKENS, D), jnp.float32)
    grad_f32 = grad_out.astype(jnp.float32)
    grads_gate, grads_up, grads_down = [], [], []
    for expert in range(EXPERTS):
        picked = (routes == expert) & kept_mask
        weight = jnp.sum(jnp.where(picked, gate_probs, jnp.zeros_like(gate_probs)), axis=1)
        at_home = jnp.any(picked & (server == 0), axis=1)[:, None]
        at_guest = jnp.any(picked & (server == 1), axis=1)[:, None]
        gate_vals = matmul(tokens, gate_full[expert])
        up_vals = matmul(tokens, up_full[expert])
        activation, slopes = silu_parts(gate_vals)
        hidden = (activation * up_vals).astype(jnp.bfloat16)
        outputs = outputs + weight[:, None] * matmul(hidden, down_full[expert])
        cotangent = (weight[:, None] * grad_f32).astype(jnp.bfloat16)
        d_hidden = matmul(cotangent, down_full[expert].T)
        d_gate = (d_hidden * up_vals * slopes).astype(jnp.bfloat16)
        d_up = (d_hidden * activation).astype(jnp.bfloat16)
        grad_tokens = grad_tokens + matmul(d_gate, gate_full[expert].T) + matmul(d_up, up_full[expert].T)
        zero_tokens = jnp.zeros_like(tokens)
        zero_hidden = jnp.zeros_like(hidden)
        home_tokens = jnp.where(at_home, tokens, zero_tokens)
        guest_tokens = jnp.where(at_guest, tokens, zero_tokens)
        home_hidden = jnp.where(at_home, hidden, zero_hidden)
        guest_hidden = jnp.where(at_guest, hidden, zero_hidden)
        grads_gate.append(split_sum(matmul(home_tokens.T, d_gate), matmul(guest_tokens.T, d_gate)))
        grads_up.append(split_sum(matmul(home_tokens.T, d_up), matmul(guest_tokens.T, d_up)))
        grads_down.append(split_sum(matmul(home_hidden.T, cotangent), matmul(guest_hidden.T, cotangent)))
    grad_gate = jnp.stack(grads_gate).reshape(EXPERTS, D, group_size, block_width).transpose(0, 2, 1, 3).reshape(EXPERTS * group_size, D, block_width)
    grad_up = jnp.stack(grads_up).reshape(EXPERTS, D, group_size, block_width).transpose(0, 2, 1, 3).reshape(EXPERTS * group_size, D, block_width)
    grad_down = jnp.stack(grads_down).reshape(EXPERTS * group_size, block_width, D)
    return outputs.astype(jnp.bfloat16), grad_tokens.astype(jnp.bfloat16), grad_gate, grad_up, grad_down
```

```python
import jax
import jax.numpy as jnp
from jax import lax
from jax.experimental import pallas as pl
from jax.experimental.pallas import tpu as pltpu
from jax.sharding import PartitionSpec as P

AXES = ("expert", "shard")
EXPERTS = 4
CAP = 6
SLOTS = 12
PAIR = 2 * SLOTS
TOK = 16
BLOCK = 4 * SLOTS
ROWS = 8 * BLOCK
WIDTH = 1024
UNITS = 384
BF16 = jnp.bfloat16
F32 = jnp.float32
MIB = 1 << 20

VMEM = pl.BlockSpec(memory_space=pltpu.VMEM)
HBM = pl.BlockSpec(memory_space=pltpu.HBM)
NT = (((1,), (1,)), ((), ()))
TN = (((0,), (0,)), ((), ()))


def send(value, flip):
    return lax.ppermute(value, AXES, [(i, flip(i)) for i in range(128)])


def over_core(value):
    return send(value, lambda i: i ^ 1)


def over_y(value, mask):
    return send(value, lambda i: i ^ (mask << 5))


def over_first(value, mask):
    return send(value, lambda i: i ^ (mask << (3 if i & 1 else 1)))


def over_second(value, mask):
    return send(value, lambda i: i ^ (mask << (1 if i & 1 else 3)))


def exchange(values, over):
    return [values[0]] + [over(values[m], m) for m in (1, 2, 3)]


def call(kernel, name, specs, shapes, operands, mib=8, scratch=(), out=None):
    spaces = {id(VMEM): pltpu.VMEM, id(HBM): pltpu.HBM}
    operands = [
        pltpu.with_memory_space_constraint(x, spaces[id(spec)]) if id(spec) in spaces else x
        for spec, x in zip(specs, operands)
    ]
    return pl.pallas_call(
        kernel,
        out_shape=[jax.ShapeDtypeStruct(s, d) if out else pltpu.VMEM(s, d) for s, d in shapes],
        in_specs=specs,
        out_specs=[out or VMEM] * len(shapes),
        scratch_shapes=list(scratch),
        compiler_params=pltpu.CompilerParams(vmem_limit_bytes=mib * MIB),
        cost_estimate=pl.CostEstimate(flops=0, bytes_accessed=0, transcendentals=0),
        name=name,
    )(*operands)


def slots_of(counts, hosted, picks, gates):
    shape = (4 * PAIR, 2 * TOK)
    row = lax.broadcasted_iota(jnp.int32, shape, 0)
    lane = lax.broadcasted_iota(jnp.int32, shape, 1)
    mask = row // PAIR
    slot = row - mask * PAIR
    expert = jnp.bitwise_xor(mask, lax.axis_index("expert") // 8)
    a = lax.broadcasted_iota(jnp.int32, (2 * TOK, 2 * TOK), 0)
    b = lax.broadcasted_iota(jnp.int32, (2 * TOK, 2 * TOK), 1)
    earlier = jnp.where((a // TOK == b // TOK) & (a < b), 1.0, 0.0)
    late = slot >= SLOTS
    wanted = jnp.where(late, slot - SLOTS, slot)
    picked = jnp.concatenate([picks, picks], axis=1)
    probs = jnp.concatenate([gates, gates], axis=1)
    first = picked[0:1] == expert
    second = picked[1:2] == expert
    has = jnp.where(first | second, 1.0, 0.0)
    weight = jnp.where(first, probs[0:1], 0.0) + jnp.where(second, probs[1:2], 0.0)
    position = jnp.dot(has.astype(BF16), earlier.astype(BF16), preferred_element_type=F32)
    position = position.astype(jnp.int32)
    limit = jnp.zeros(shape, jnp.int32)
    for e in range(EXPERTS):
        quota = jnp.minimum((counts[e] + 63) // 64, CAP)
        limit = jnp.where(expert == e, quota + hosted[e ^ 1], limit)
    hit = (has > 0.5) & (position < limit) & (position == wanted) & (late == (lane >= TOK))
    return jnp.where(hit, 1.0, 0.0), late, weight


ROUTING = [
    pltpu.SMEM((EXPERTS,), jnp.int32),
    pltpu.SMEM((EXPERTS,), jnp.int32),
    pltpu.VMEM((2, TOK), jnp.int32),
    pltpu.VMEM((2, TOK), F32),
]


def fetch(sources, targets, sems):
    copies = [pltpu.make_async_copy(s, t, sems.at[i]) for i, (s, t) in enumerate(zip(sources, targets))]
    for copy in copies:
        copy.start()
    return copies


def pack(routing, tokens, grad_out):
    def kernel(*refs):
        sources, outs, (counts, hosted, picks, gates, values, sems) = refs[:6], refs[6:10], refs[10:]
        targets = [counts, hosted, picks, gates, values.at[:TOK], values.at[TOK:]]
        for copy in fetch(sources, targets, sems):
            copy.wait()
        one_hot, late, weight = slots_of(counts, hosted, picks[...], gates[...])
        scale = jnp.sum(jnp.where(late, one_hot * weight, one_hot), axis=1, keepdims=True)
        rows = jnp.dot(one_hot.astype(BF16), values[...], preferred_element_type=F32) * scale
        for m in range(4):
            outs[m][...] = rows[m * PAIR : (m + 1) * PAIR].astype(BF16)

    scratch = ROUTING + [pltpu.VMEM((2 * TOK, WIDTH), BF16), pltpu.SemaphoreType.DMA((6,))]
    shapes = [((PAIR, WIDTH), BF16)] * 4
    return call(kernel, "pack", [HBM] * 6, shapes, (*routing, tokens, grad_out), scratch=scratch)


def combine_matrix(routing):
    def kernel(*refs):
        sources, out, targets, sems = refs[:4], refs[4], refs[5:9], refs[9]
        for copy in fetch(sources, targets, sems):
            copy.wait()
        counts, hosted, picks, gates = targets
        one_hot, late, weight = slots_of(counts, hosted, picks[...], gates[...])
        out[...] = jnp.where(late, one_hot, one_hot * weight)

    scratch = ROUTING + [pltpu.SemaphoreType.DMA((4,))]
    return call(kernel, "combine_matrix", [HBM] * 4, [((4 * PAIR, 2 * TOK), F32)], routing, scratch=scratch)[0]


def join_y(parts):
    total = 4 * PAIR

    def kernel(a, b, c, d, out):
        stacked = jnp.concatenate([p[...].astype(F32) for p in (a, b, c, d)], axis=0).astype(BF16)
        to = lax.broadcasted_iota(jnp.int32, (total, total), 0)
        come = lax.broadcasted_iota(jnp.int32, (total, total), 1)
        half = to // BLOCK
        inner = to - half * BLOCK
        source = inner // SLOTS
        wanted = source * PAIR + half * SLOTS + (inner - source * SLOTS)
        order = jnp.where(come == wanted, 1.0, 0.0).astype(BF16)
        out[...] = jnp.dot(order, stacked, preferred_element_type=F32).astype(BF16)

    return call(kernel, "join_y", [VMEM] * 4, [((total, WIDTH), BF16)], parts)[0]


def load_weights(w_gate, w_up, w_down):
    def kernel(wg, wu, wd, both, down, sems):
        targets = [both.at[:, :UNITS], both.at[:, UNITS:], down]
        for copy in fetch([wg.at[0], wu.at[0], wd.at[0]], targets, sems):
            copy.wait()

    shapes = [((4 * WIDTH, 2 * UNITS), BF16), ((UNITS, 4 * WIDTH), BF16)]
    scratch = [pltpu.SemaphoreType.DMA((3,))]
    return call(kernel, "load_weights", [HBM] * 3, shapes, (w_gate, w_up, w_down), scratch=scratch)


def join_first(parts):
    def kernel(a, b, c, d, out):
        for m, part in enumerate((a, b, c, d)):
            out[m] = part[...]

    return call(kernel, "join_first", [VMEM] * 4, [((4, 2 * BLOCK, WIDTH), BF16)], parts)[0]


def join_second(parts, half):
    def kernel(a, b, c, d, out):
        for m, part in enumerate((a, b, c, d)):
            out[m] = part[:, half * BLOCK : (half + 1) * BLOCK, :]

    return call(kernel, f"join_second_{half}", [VMEM] * 4, [((4, 4, BLOCK, WIDTH), BF16)], parts)[0]


def place(core, xlm, zm, xhm):
    xm = xhm * 2 + xlm
    return jnp.where(core == 0, zm, xm), jnp.where(core == 0, xm, zm)


def rows_of(core, xlm, pieces):
    blocks = [pieces[place(core, xlm, zm, xhm)] for zm in range(4) for xhm in range(2)]
    return jnp.concatenate(blocks, axis=0)


def scatter_rows(core, xlm, rows, out_ref):
    for zm in range(4):
        for xhm in range(2):
            row = (zm * 2 + xhm) * BLOCK
            out_ref[place(core, xlm, zm, xhm)] = rows[row : row + BLOCK].astype(out_ref.dtype)


def at(shard, fm):
    return pl.ds(pl.multiple_of(jnp.bitwise_xor(shard, fm) * WIDTH, WIDTH), WIDTH)


def forward(cm, pieces, w_both, before):
    def kernel(pieces, w, *refs):
        shard = lax.axis_index("shard")
        total, both_ref = None if before is None else refs[0][...], refs[0 if before is None else 1]
        for xlm in range(2):
            rows = rows_of((shard & 1) ^ cm, xlm, pieces)
            part = jnp.dot(rows, w[at(shard, xlm * 2 + cm), :], preferred_element_type=F32)
            total = part if total is None else total + part
        both_ref[...] = total
        if before is not None:
            gate = both_ref[:, :UNITS]
            refs[2][...] = (gate * jax.nn.sigmoid(gate) * both_ref[:, UNITS:]).astype(BF16)

    shapes = [((ROWS, 2 * UNITS), F32)]
    specs, operands = [VMEM, VMEM], (pieces, w_both)
    if before is not None:
        shapes, specs, operands = shapes + [((ROWS, UNITS), BF16)], specs + [VMEM], operands + (before,)
    return call(kernel, f"forward_{cm}", specs, shapes, operands, 8)


def out_rows(cm, hidden, w_down):
    def kernel(hidden, w, out_ref):
        shard = lax.axis_index("shard")
        for xlm in range(2):
            rows = jnp.dot(hidden[...], w[:, at(shard, xlm * 2 + cm)], preferred_element_type=F32)
            scatter_rows((shard & 1) ^ cm, xlm, rows, out_ref)

    shapes = [((4, 4, BLOCK, WIDTH), BF16)]
    return call(kernel, f"out_rows_{cm}", [VMEM, VMEM], shapes, (hidden, w_down))[0]


def backward_hidden(cm, pieces, w_down, before, both):
    def kernel(pieces, w, *refs):
        shard = lax.axis_index("shard")
        total = None if before is None else refs[0][...]
        for xlm in range(2):
            rows = rows_of((shard & 1) ^ cm, xlm, pieces)
            part = lax.dot_general(rows, w[:, at(shard, xlm * 2 + cm)], NT, preferred_element_type=F32)
            total = part if total is None else total + part
        if before is None:
            refs[0][...] = total
            return
        both_ref, d_ref = refs[1:]
        gate, up = both_ref[:, :UNITS], both_ref[:, UNITS:]
        sigma = jax.nn.sigmoid(gate)
        d_ref[:, :UNITS] = (total * up * (sigma * (1.0 + gate * (1.0 - sigma)))).astype(BF16)
        d_ref[:, UNITS:] = (total * (gate * sigma)).astype(BF16)

    name, specs, operands = f"backward_hidden_{cm}", [VMEM, VMEM], (pieces, w_down)
    if before is None:
        return call(kernel, name, specs, [((ROWS, UNITS), F32)], operands)[0]
    shapes = [((ROWS, 2 * UNITS), BF16)]
    return call(kernel, name, specs + [VMEM] * 2, shapes, operands + (before, both))[0]


def back_rows(cm, d_both, w_both):
    def kernel(d, w, out_ref):
        shard = lax.axis_index("shard")
        for xlm in range(2):
            rows = lax.dot_general(d[...], w[at(shard, xlm * 2 + cm), :], NT, preferred_element_type=F32)
            scatter_rows((shard & 1) ^ cm, xlm, rows, out_ref)

    shapes = [((4, 4, BLOCK, WIDTH), BF16)]
    return call(kernel, f"back_rows_{cm}", [VMEM, VMEM], shapes, (d_both, w_both))[0]


def gate_up_grads(x_pieces, d_both):
    def kernel(mine, theirs, d, gate_out, up_out, total, sems):
        shard = lax.axis_index("shard")
        copies = [None] * 4
        for fm in range(4):
            slot = fm % 2
            if fm >= 2:
                wait_all(copies[fm - 2])
            rows = rows_of((shard & 1) ^ (fm % 2), fm // 2, theirs if fm % 2 else mine)
            total[slot] = lax.dot_general(rows, d[...], TN, preferred_element_type=F32).astype(BF16)
            sources = [total.at[slot, :, :UNITS], total.at[slot, :, UNITS:]]
            targets = [gate_out.at[0, at(shard, fm), :], up_out.at[0, at(shard, fm), :]]
            copies[fm] = fetch(sources, targets, sems.at[slot])
        wait_all(copies[2])
        wait_all(copies[3])

    shapes = [((1, 4 * WIDTH, UNITS), BF16)] * 2
    scratch = [pltpu.VMEM((2, WIDTH, 2 * UNITS), BF16), pltpu.SemaphoreType.DMA((2, 2))]
    operands = (*x_pieces, d_both)
    return call(kernel, "gate_up_grads", [VMEM] * 3, shapes, operands, 12, scratch, HBM)


def down_grad(cot_pieces, hidden):
    def kernel(mine, theirs, hidden, out, total, sems):
        shard = lax.axis_index("shard")
        copies = [None] * 4
        for fm in range(4):
            slot = fm % 2
            if fm >= 2:
                wait_all(copies[fm - 2])
            rows = rows_of((shard & 1) ^ (fm % 2), fm // 2, theirs if fm % 2 else mine)
            total[slot] = lax.dot_general(hidden[...], rows, TN, preferred_element_type=F32).astype(BF16)
            copies[fm] = fetch([total.at[slot]], [out.at[0, :, at(shard, fm)]], sems.at[slot])
        wait_all(copies[2])
        wait_all(copies[3])

    shapes = [((1, UNITS, 4 * WIDTH), BF16)]
    scratch = [pltpu.VMEM((2, UNITS, WIDTH), BF16), pltpu.SemaphoreType.DMA((2, 1))]
    operands = (*cot_pieces, hidden)
    return call(kernel, "down_grad", [VMEM] * 3, shapes, operands, 10, scratch, HBM)[0]


def wait_all(copies):
    for copy in copies:
        copy.wait()


def sum_cores(mine, theirs):
    def kernel(a, b, *outs):
        for m in range(4):
            outs[m][...] = (a[m].astype(F32) + b[m].astype(F32)).astype(BF16)

    return call(kernel, "sum_cores", [VMEM] * 2, [((4, BLOCK, WIDTH), BF16)] * 4, (mine, theirs))


def sum_second(pieces):
    def kernel(a, b, c, d, *outs):
        for m in range(4):
            total = (a[m].astype(F32) + b[m].astype(F32)) + (c[m].astype(F32) + d[m].astype(F32))
            outs[m][...] = total.astype(outs[m].dtype)

    shapes = [((BLOCK, WIDTH), F32)] + [((BLOCK, WIDTH), BF16)] * 3
    return call(kernel, "sum_second", [VMEM] * 4, shapes, pieces)


def sum_second_both(blocks, pieces):
    def kernel(*refs):
        (a, b, c, d), outs = refs[4:8], refs[8:]
        for m in range(4):
            total = (a[m].astype(F32) + b[m].astype(F32)) + (c[m].astype(F32) + d[m].astype(F32))
            outs[m][:BLOCK, :] = refs[m][...]
            outs[m][BLOCK:, :] = total.astype(outs[m].dtype)

    shapes = [((2 * BLOCK, WIDTH), F32)] + [((2 * BLOCK, WIDTH), BF16)] * 3
    return call(kernel, "sum_second_both", [VMEM] * 8, shapes, (*blocks, *pieces))


def sum_first(blocks):
    def kernel(a, b, c, d, *outs):
        total = (a[...] + b[...].astype(F32)) + (c[...].astype(F32) + d[...].astype(F32))
        for m in range(4):
            for half in range(2):
                row = half * BLOCK + m * SLOTS
                outs[m][half * SLOTS : (half + 1) * SLOTS, :] = total[row : row + SLOTS]

    return call(kernel, "sum_first", [VMEM] * 4, [((PAIR, WIDTH), F32)] * 4, blocks)


def combine(matrix, parts):
    def kernel(matrix, a, b, c, d, outputs, grads):
        stacked = jnp.concatenate([p[...] for p in (a, b, c, d)], axis=0)
        total = lax.dot_general(
            matrix[...], stacked, TN, precision=lax.Precision.HIGHEST, preferred_element_type=F32
        )
        outputs[...] = total[:TOK].astype(BF16)
        grads[...] = total[TOK:].astype(BF16)

    return call(kernel, "combine", [VMEM] * 5, [((TOK, WIDTH), BF16)] * 2, (matrix, *parts), out=VMEM)


def per_device(tokens, routes, gate_probs, prev_counts, hosts, w_gate, w_up, w_down, grad_out):
    routing = (prev_counts, hosts, routes.T, gate_probs.T)
    tie = lax.optimization_barrier
    payload = exchange(pack(routing, tokens, grad_out), over_y)
    payload, matrix, (w_both, w_down) = tie(
        (payload, combine_matrix(routing), load_weights(w_gate, w_up, w_down))
    )
    both = join_first(exchange([join_y(payload)] * 4, over_first))
    both = exchange([both] * 4, over_second)
    x_mine = join_second(both, 0)
    x_theirs = over_core(x_mine)
    cot_mine = join_second(both, 1)
    cot_theirs = over_core(cot_mine)

    (part,) = forward(0, x_mine, w_both, None)
    back_part = backward_hidden(0, cot_mine, w_down, None, None)
    gate_up, hidden = forward(1, x_theirs, w_both, part)
    d_both = backward_hidden(1, cot_theirs, w_down, back_part, gate_up)
    back_theirs = over_core(back_rows(1, d_both, w_both))
    back_mine = back_rows(0, d_both, w_both)
    back_pieces = exchange(sum_cores(back_mine, back_theirs), over_second)
    out_theirs = over_core(out_rows(1, hidden, w_down))
    out_mine = out_rows(0, hidden, w_down)
    out_pieces = exchange(sum_cores(out_mine, out_theirs), over_second)
    grads = (
        *gate_up_grads((x_mine, x_theirs), d_both),
        down_grad((cot_mine, cot_theirs), hidden),
    )
    back_pieces, out_pieces, grads = tie((back_pieces, out_pieces, grads))
    blocks = exchange(sum_second_both(sum_second(out_pieces), back_pieces), over_first)
    parts = exchange(sum_first(blocks), over_y)
    outputs, grad_tokens = combine(matrix, parts)
    return outputs, grad_tokens, *grads


def solution(mesh):
    rows, weights = P("expert", "shard"), P("expert", None, "shard")
    down = P("expert", "shard", None)
    small = P("expert", None)
    return jax.shard_map(
        per_device,
        mesh=mesh,
        in_specs=(rows, small, small, P(), P(), weights, weights, down, rows),
        out_specs=(rows, rows, weights, weights, down),
        check_vma=False,
    )
```

```python
import jax
import jax.numpy as jnp
from jax import lax
from jax.experimental import pallas as pl
from jax.experimental.pallas import tpu as pltpu
from jax.sharding import PartitionSpec as P

AXES = ("expert", "shard")
EXPERTS = 4
CAP = 6
SLOTS = 12
PAIR = 2 * SLOTS
TOK = 16
BLOCK = 4 * SLOTS
ROWS = 8 * BLOCK
WIDTH = 1024
UNITS = 384
BF16 = jnp.bfloat16
F32 = jnp.float32
MIB = 1 << 20

VMEM = pl.BlockSpec(memory_space=pltpu.VMEM)
HBM = pl.BlockSpec(memory_space=pltpu.HBM)
NT = (((1,), (1,)), ((), ()))
TN = (((0,), (0,)), ((), ()))


def send(value, flip):
    return lax.ppermute(value, AXES, [(i, flip(i)) for i in range(128)])


def over_core(value):
    return send(value, lambda i: i ^ 1)


def over_y(value, mask):
    return send(value, lambda i: i ^ (mask << 5))


def over_first(value, mask):
    return send(value, lambda i: i ^ (mask << (3 if i & 1 else 1)))


def over_second(value, mask):
    return send(value, lambda i: i ^ (mask << (1 if i & 1 else 3)))


ORDER = (0, 3, 2, 1)


def exchange(values, over):
    return [values[0]] + [over(values[m], m) for m in ORDER[1:]]


def call(kernel, name, specs, shapes, operands, mib=8, scratch=(), out=None):
    spaces = {id(VMEM): pltpu.VMEM, id(HBM): pltpu.HBM}
    operands = [
        pltpu.with_memory_space_constraint(x, spaces[id(spec)]) if id(spec) in spaces else x
        for spec, x in zip(specs, operands)
    ]
    return pl.pallas_call(
        kernel,
        out_shape=[jax.ShapeDtypeStruct(s, d) if out else pltpu.VMEM(s, d) for s, d in shapes],
        in_specs=specs,
        out_specs=[out or VMEM] * len(shapes),
        scratch_shapes=list(scratch),
        compiler_params=pltpu.CompilerParams(vmem_limit_bytes=mib * MIB),
        cost_estimate=pl.CostEstimate(flops=0, bytes_accessed=0, transcendentals=0),
        name=name,
    )(*operands)


def slots_of(counts, hosted, picks, gates):
    shape = (4 * PAIR, 2 * TOK)
    row = lax.broadcasted_iota(jnp.int32, shape, 0)
    lane = lax.broadcasted_iota(jnp.int32, shape, 1)
    mask = row // PAIR
    slot = row - mask * PAIR
    expert = jnp.bitwise_xor(mask, lax.axis_index("expert") // 8)
    a = lax.broadcasted_iota(jnp.int32, (2 * TOK, 2 * TOK), 0)
    b = lax.broadcasted_iota(jnp.int32, (2 * TOK, 2 * TOK), 1)
    earlier = jnp.where((a // TOK == b // TOK) & (a < b), 1.0, 0.0)
    late = slot >= SLOTS
    wanted = jnp.where(late, slot - SLOTS, slot)
    picked = jnp.concatenate([picks, picks], axis=1)
    probs = jnp.concatenate([gates, gates], axis=1)
    first = picked[0:1] == expert
    second = picked[1:2] == expert
    has = jnp.where(first | second, 1.0, 0.0)
    weight = jnp.where(first, probs[0:1], 0.0) + jnp.where(second, probs[1:2], 0.0)
    position = jnp.dot(has.astype(BF16), earlier.astype(BF16), preferred_element_type=F32)
    position = position.astype(jnp.int32)
    limit = jnp.zeros(shape, jnp.int32)
    for e in range(EXPERTS):
        quota = jnp.minimum((counts[e] + 63) // 64, CAP)
        limit = jnp.where(expert == e, quota + hosted[e ^ 1], limit)
    hit = (has > 0.5) & (position < limit) & (position == wanted) & (late == (lane >= TOK))
    return jnp.where(hit, 1.0, 0.0), late, weight


ROUTING = [
    pltpu.SMEM((EXPERTS,), jnp.int32),
    pltpu.SMEM((EXPERTS,), jnp.int32),
    pltpu.VMEM((2, TOK), jnp.int32),
    pltpu.VMEM((2, TOK), F32),
]


def fetch(sources, targets, sems):
    copies = [pltpu.make_async_copy(s, t, sems.at[i]) for i, (s, t) in enumerate(zip(sources, targets))]
    for copy in copies:
        copy.start()
    return copies


def pack(routing, tokens, grad_out):
    def kernel(*refs):
        sources, outs, (counts, hosted, picks, gates, values, sems) = refs[:6], refs[6:10], refs[10:]
        targets = [counts, hosted, picks, gates, values.at[:TOK], values.at[TOK:]]
        for copy in fetch(sources, targets, sems):
            copy.wait()
        one_hot, late, weight = slots_of(counts, hosted, picks[...], gates[...])
        scale = jnp.sum(jnp.where(late, one_hot * weight, one_hot), axis=1, keepdims=True)
        rows = jnp.dot(one_hot.astype(BF16), values[...], preferred_element_type=F32) * scale
        for m in range(4):
            outs[m][...] = rows[m * PAIR : (m + 1) * PAIR].astype(BF16)

    scratch = ROUTING + [pltpu.VMEM((2 * TOK, WIDTH), BF16), pltpu.SemaphoreType.DMA((6,))]
    shapes = [((PAIR, WIDTH), BF16)] * 4
    return call(kernel, "pack", [HBM] * 6, shapes, (*routing, tokens, grad_out), scratch=scratch)


def combine_matrix(routing):
    def kernel(*refs):
        sources, out, targets, sems = refs[:4], refs[4], refs[5:9], refs[9]
        for copy in fetch(sources, targets, sems):
            copy.wait()
        counts, hosted, picks, gates = targets
        one_hot, late, weight = slots_of(counts, hosted, picks[...], gates[...])
        out[...] = jnp.where(late, one_hot, one_hot * weight)

    scratch = ROUTING + [pltpu.SemaphoreType.DMA((4,))]
    return call(kernel, "combine_matrix", [HBM] * 4, [((4 * PAIR, 2 * TOK), F32)], routing, scratch=scratch)[0]


def join_y(parts):
    total = 4 * PAIR

    def kernel(a, d, c, b, out):
        stacked = jnp.concatenate([p[...].astype(F32) for p in (a, b, c, d)], axis=0).astype(BF16)
        to = lax.broadcasted_iota(jnp.int32, (total, total), 0)
        come = lax.broadcasted_iota(jnp.int32, (total, total), 1)
        half = to // BLOCK
        inner = to - half * BLOCK
        source = inner // SLOTS
        wanted = source * PAIR + half * SLOTS + (inner - source * SLOTS)
        order = jnp.where(come == wanted, 1.0, 0.0).astype(BF16)
        out[...] = jnp.dot(order, stacked, preferred_element_type=F32).astype(BF16)

    return call(kernel, "join_y", [VMEM] * 4, [((total, WIDTH), BF16)], parts)[0]


def load_weights(w_gate, w_up, w_down):
    def kernel(wg, wu, wd, both, down, sems):
        targets = [both.at[:, :UNITS], both.at[:, UNITS:], down]
        for copy in fetch([wg.at[0], wu.at[0], wd.at[0]], targets, sems):
            copy.wait()

    shapes = [((4 * WIDTH, 2 * UNITS), BF16), ((UNITS, 4 * WIDTH), BF16)]
    scratch = [pltpu.SemaphoreType.DMA((3,))]
    return call(kernel, "load_weights", [HBM] * 3, shapes, (w_gate, w_up, w_down), scratch=scratch)


def join_first(parts):
    def kernel(a, d, c, b, x_out, cot_out):
        for m, part in enumerate((a, b, c, d)):
            x_out[m] = part[:BLOCK, :]
            cot_out[m] = part[BLOCK:, :]

    return call(kernel, "join_first", [VMEM] * 4, [((4, BLOCK, WIDTH), BF16)] * 2, parts)


def join_second(parts):
    def kernel(a, d, c, b, out):
        for m, part in enumerate((a, b, c, d)):
            out[m] = part[...]

    return call(kernel, "join_second", [VMEM] * 4, [((4, 4, BLOCK, WIDTH), BF16)], parts)[0]


def place(core, xlm, zm, xhm):
    xm = xhm * 2 + xlm
    return jnp.where(core == 0, zm, xm), jnp.where(core == 0, xm, zm)


def rows_of(core, xlm, pieces):
    blocks = [pieces[place(core, xlm, zm, xhm)] for zm in range(4) for xhm in range(2)]
    return jnp.concatenate(blocks, axis=0)


def scatter_rows(core, xlm, rows, out_ref):
    for zm in range(4):
        for xhm in range(2):
            row = (zm * 2 + xhm) * BLOCK
            out_ref[place(core, xlm, zm, xhm)] = rows[row : row + BLOCK].astype(out_ref.dtype)


def at(shard, fm):
    return pl.ds(pl.multiple_of(jnp.bitwise_xor(shard, fm) * WIDTH, WIDTH), WIDTH)


def forward(cm, pieces, w_both, before):
    def kernel(pieces, w, *refs):
        shard = lax.axis_index("shard")
        total, both_ref = None if before is None else refs[0][...], refs[0 if before is None else 1]
        for xlm in range(2):
            rows = rows_of((shard & 1) ^ cm, xlm, pieces)
            part = jnp.dot(rows, w[at(shard, xlm * 2 + cm), :], preferred_element_type=F32)
            total = part if total is None else total + part
        both_ref[...] = total
        if before is not None:
            gate = both_ref[:, :UNITS]
            refs[2][...] = (gate * jax.nn.sigmoid(gate) * both_ref[:, UNITS:]).astype(BF16)

    shapes = [((ROWS, 2 * UNITS), F32)]
    specs, operands = [VMEM, VMEM], (pieces, w_both)
    if before is not None:
        shapes, specs, operands = shapes + [((ROWS, UNITS), BF16)], specs + [VMEM], operands + (before,)
    return call(kernel, f"forward_{cm}", specs, shapes, operands, 8)


def out_rows(cm, hidden, w_down):
    def kernel(hidden, w, out_ref):
        shard = lax.axis_index("shard")
        for xlm in range(2):
            rows = jnp.dot(hidden[...], w[:, at(shard, xlm * 2 + cm)], preferred_element_type=F32)
            scatter_rows((shard & 1) ^ cm, xlm, rows, out_ref)

    shapes = [((4, 4, BLOCK, WIDTH), BF16)]
    return call(kernel, f"out_rows_{cm}", [VMEM, VMEM], shapes, (hidden, w_down))[0]


def backward_hidden(cm, pieces, w_down, before, both):
    def kernel(pieces, w, *refs):
        shard = lax.axis_index("shard")
        total = None if before is None else refs[0][...]
        for xlm in range(2):
            rows = rows_of((shard & 1) ^ cm, xlm, pieces)
            part = lax.dot_general(rows, w[:, at(shard, xlm * 2 + cm)], NT, preferred_element_type=F32)
            total = part if total is None else total + part
        if before is None:
            refs[0][...] = total
            return
        both_ref, d_ref = refs[1:]
        gate, up = both_ref[:, :UNITS], both_ref[:, UNITS:]
        sigma = jax.nn.sigmoid(gate)
        d_ref[:, :UNITS] = (total * up * (sigma * (1.0 + gate * (1.0 - sigma)))).astype(BF16)
        d_ref[:, UNITS:] = (total * (gate * sigma)).astype(BF16)

    name, specs, operands = f"backward_hidden_{cm}", [VMEM, VMEM], (pieces, w_down)
    if before is None:
        return call(kernel, name, specs, [((ROWS, UNITS), F32)], operands)[0]
    shapes = [((ROWS, 2 * UNITS), BF16)]
    return call(kernel, name, specs + [VMEM] * 2, shapes, operands + (before, both))[0]


def back_rows(cm, d_both, w_both):
    def kernel(d, w, out_ref):
        shard = lax.axis_index("shard")
        for xlm in range(2):
            rows = lax.dot_general(d[...], w[at(shard, xlm * 2 + cm), :], NT, preferred_element_type=F32)
            scatter_rows((shard & 1) ^ cm, xlm, rows, out_ref)

    shapes = [((4, 4, BLOCK, WIDTH), BF16)]
    return call(kernel, f"back_rows_{cm}", [VMEM, VMEM], shapes, (d_both, w_both))[0]


def weight_grads(x_pieces, cot_pieces, d_both, hidden):
    def kernel(x_mine, x_theirs, cot_mine, cot_theirs, d, hidden, gate_out, up_out, down_out, both, down, sems):
        shard = lax.axis_index("shard")
        copies = []
        for fm in range(4):
            side = (shard & 1) ^ (fm % 2)
            if fm >= 2:
                wait_all(copies[fm - 2])
            slot = fm % 2
            rows = rows_of(side, fm // 2, x_theirs if fm % 2 else x_mine)
            both[slot] = lax.dot_general(rows, d[...], TN, preferred_element_type=F32).astype(BF16)
            sources = [both.at[slot, :, :UNITS], both.at[slot, :, UNITS:]]
            targets = [gate_out.at[0, at(shard, fm), :], up_out.at[0, at(shard, fm), :]]
            started = fetch(sources, targets, sems.at[slot])
            rows = rows_of(side, fm // 2, cot_theirs if fm % 2 else cot_mine)
            down[slot] = lax.dot_general(hidden[...], rows, TN, preferred_element_type=F32).astype(BF16)
            last = pltpu.make_async_copy(down.at[slot], down_out.at[0, :, at(shard, fm)], sems.at[slot, 2])
            last.start()
            copies.append(started + [last])
        wait_all(copies[2])
        wait_all(copies[3])

    shapes = [((1, 4 * WIDTH, UNITS), BF16)] * 2 + [((1, UNITS, 4 * WIDTH), BF16)]
    scratch = [
        pltpu.VMEM((2, WIDTH, 2 * UNITS), BF16),
        pltpu.VMEM((2, UNITS, WIDTH), BF16),
        pltpu.SemaphoreType.DMA((2, 3)),
    ]
    operands = (*x_pieces, *cot_pieces, d_both, hidden)
    return call(kernel, "weight_grads", [VMEM] * 6, shapes, operands, 14, scratch, HBM)


def wait_all(copies):
    for copy in copies:
        copy.wait()


def sum_cores(mine, theirs):
    def kernel(a, b, *outs):
        for m in range(4):
            outs[m][...] = (a[m].astype(F32) + b[m].astype(F32)).astype(BF16)

    return call(kernel, "sum_cores", [VMEM] * 2, [((4, BLOCK, WIDTH), BF16)] * 4, (mine, theirs))


def sum_second(pieces):
    def kernel(a, d, c, b, *outs):
        for m in range(4):
            total = (a[m].astype(F32) + b[m].astype(F32)) + (c[m].astype(F32) + d[m].astype(F32))
            outs[m][...] = total.astype(outs[m].dtype)

    shapes = [((BLOCK, WIDTH), F32)] + [((BLOCK, WIDTH), BF16)] * 3
    return call(kernel, "sum_second", [VMEM] * 4, shapes, pieces)


def sum_second_both(blocks, pieces):
    def kernel(*refs):
        (a, b, c, d), outs = refs[4:8], refs[8:]
        for m in range(4):
            total = (a[m].astype(F32) + b[m].astype(F32)) + (c[m].astype(F32) + d[m].astype(F32))
            outs[m][:BLOCK, :] = refs[m][...]
            outs[m][BLOCK:, :] = total.astype(outs[m].dtype)

    shapes = [((2 * BLOCK, WIDTH), F32)] + [((2 * BLOCK, WIDTH), BF16)] * 3
    return call(kernel, "sum_second_both", [VMEM] * 8, shapes, (*blocks, *pieces))


def sum_first(blocks):
    def kernel(a, d, c, b, *outs):
        total = (a[...] + b[...].astype(F32)) + (c[...].astype(F32) + d[...].astype(F32))
        for m in range(4):
            halves = [total[half * BLOCK + m * SLOTS :][:SLOTS] for half in range(2)]
            outs[m][...] = jnp.concatenate(halves, axis=0).astype(outs[m].dtype)

    shapes = [((PAIR, WIDTH), F32)] + [((PAIR, WIDTH), BF16)] * 3
    return call(kernel, "sum_first", [VMEM] * 4, shapes, blocks)


def combine(matrix, parts):
    def kernel(matrix, a, d, c, b, outputs, grads):
        stacked = jnp.concatenate([p[...].astype(F32) for p in (a, b, c, d)], axis=0)
        total = lax.dot_general(
            matrix[...], stacked, TN, precision=lax.Precision.HIGHEST, preferred_element_type=F32
        )
        outputs[...] = total[:TOK].astype(BF16)
        grads[...] = total[TOK:].astype(BF16)

    return call(kernel, "combine", [VMEM] * 5, [((TOK, WIDTH), BF16)] * 2, (matrix, *parts), out=VMEM)


def per_device(tokens, routes, gate_probs, prev_counts, hosts, w_gate, w_up, w_down, grad_out):
    routing = (prev_counts, hosts, routes.T, gate_probs.T)
    tie = lax.optimization_barrier
    payload = exchange(pack(routing, tokens, grad_out), over_y)
    payload, matrix = tie((payload, combine_matrix(routing)))
    both, (w_both, w_down) = tie(
        (exchange([join_y(payload)] * 4, over_first), load_weights(w_gate, w_up, w_down))
    )
    x_quarter, cot_quarter = join_first(both)
    x_quarters = exchange([x_quarter] * 4, over_second)
    x_mine = join_second(x_quarters)
    x_theirs = [over_core(x) for x in x_quarters]
    cot_mine = join_second(exchange([cot_quarter] * 4, over_second))
    (part,) = forward(0, x_mine, w_both, None)
    x_theirs, cot_mine, part = tie((x_theirs, cot_mine, part))
    x_theirs = join_second(x_theirs)
    cot_theirs = over_core(cot_mine)
    gate_up, hidden = forward(1, x_theirs, w_both, part)
    out_theirs = over_core(out_rows(1, hidden, w_down))
    part = backward_hidden(0, cot_mine, w_down, None, None)
    d_both = backward_hidden(1, cot_theirs, w_down, part, gate_up)
    back_theirs = over_core(back_rows(1, d_both, w_both))
    out_pieces = exchange(sum_cores(out_rows(0, hidden, w_down), out_theirs), over_second)
    back_pieces = exchange(sum_cores(back_rows(0, d_both, w_both), back_theirs), over_second)
    grads = weight_grads((x_mine, x_theirs), (cot_mine, cot_theirs), d_both, hidden)
    back_pieces, out_pieces, grads = tie((back_pieces, out_pieces, grads))
    blocks = exchange(sum_second_both(sum_second(out_pieces), back_pieces), over_first)
    parts = exchange(sum_first(blocks), over_y)
    outputs, grad_tokens = combine(matrix, parts)
    return outputs, grad_tokens, *grads


def solution(mesh):
    rows, weights = P("expert", "shard"), P("expert", None, "shard")
    down = P("expert", "shard", None)
    small = P("expert", None)
    return jax.shard_map(
        per_device,
        mesh=mesh,
        in_specs=(rows, small, small, P(), P(), weights, weights, down, rows),
        out_specs=(rows, rows, weights, weights, down),
        check_vma=False,
    )
```

```python
import jax
import jax.numpy as jnp
from jax import lax
from jax.experimental import pallas as pl
from jax.experimental.pallas import tpu as pltpu
from jax.sharding import PartitionSpec as P

AXES = ("expert", "shard")
EXPERTS = 4
CAP = 6
SLOTS = 12
PAIR = 2 * SLOTS
TOK = 16
BLOCK = 4 * SLOTS
ROWS = 8 * BLOCK
WIDTH = 1024
UNITS = 384
BF16 = jnp.bfloat16
F32 = jnp.float32
MIB = 1 << 20

VMEM = pl.BlockSpec(memory_space=pltpu.VMEM)
HBM = pl.BlockSpec(memory_space=pltpu.HBM)
NT = (((1,), (1,)), ((), ()))
TN = (((0,), (0,)), ((), ()))


def send(value, flip):
    return lax.ppermute(value, AXES, [(i, flip(i)) for i in range(128)])


def over_core(value):
    return send(value, lambda i: i ^ 1)


def over_y(value, mask):
    return send(value, lambda i: i ^ (mask << 5))


def over_first(value, mask):
    return send(value, lambda i: i ^ (mask << (3 if i & 1 else 1)))


def over_second(value, mask):
    return send(value, lambda i: i ^ (mask << (1 if i & 1 else 3)))


ORDER = (0, 2, 3, 1)


def exchange(values, over):
    return [values[0]] + [over(values[m], m) for m in ORDER[1:]]


def call(kernel, name, specs, shapes, operands, mib=8, scratch=(), out=None):
    spaces = {id(VMEM): pltpu.VMEM, id(HBM): pltpu.HBM}
    operands = [
        pltpu.with_memory_space_constraint(x, spaces[id(spec)]) if id(spec) in spaces else x
        for spec, x in zip(specs, operands)
    ]
    return pl.pallas_call(
        kernel,
        out_shape=[jax.ShapeDtypeStruct(s, d) if out else pltpu.VMEM(s, d) for s, d in shapes],
        in_specs=specs,
        out_specs=[out or VMEM] * len(shapes),
        scratch_shapes=list(scratch),
        compiler_params=pltpu.CompilerParams(vmem_limit_bytes=mib * MIB),
        cost_estimate=pl.CostEstimate(flops=0, bytes_accessed=0, transcendentals=0),
        name=name,
    )(*operands)


def slots_of(counts, hosted, picks, gates):
    shape = (4 * PAIR, 2 * TOK)
    row = lax.broadcasted_iota(jnp.int32, shape, 0)
    lane = lax.broadcasted_iota(jnp.int32, shape, 1)
    mask = row // PAIR
    slot = row - mask * PAIR
    expert = jnp.bitwise_xor(mask, lax.axis_index("expert") // 8)
    a = lax.broadcasted_iota(jnp.int32, (2 * TOK, 2 * TOK), 0)
    b = lax.broadcasted_iota(jnp.int32, (2 * TOK, 2 * TOK), 1)
    earlier = jnp.where((a // TOK == b // TOK) & (a < b), 1.0, 0.0)
    late = slot >= SLOTS
    wanted = jnp.where(late, slot - SLOTS, slot)
    picked = jnp.concatenate([picks, picks], axis=1)
    probs = jnp.concatenate([gates, gates], axis=1)
    first = picked[0:1] == expert
    second = picked[1:2] == expert
    has = jnp.where(first | second, 1.0, 0.0)
    weight = jnp.where(first, probs[0:1], 0.0) + jnp.where(second, probs[1:2], 0.0)
    position = jnp.dot(has.astype(BF16), earlier.astype(BF16), preferred_element_type=F32)
    position = position.astype(jnp.int32)
    limit = jnp.zeros(shape, jnp.int32)
    for e in range(EXPERTS):
        quota = jnp.minimum((counts[e] + 63) // 64, CAP)
        limit = jnp.where(expert == e, quota + hosted[e ^ 1], limit)
    hit = (has > 0.5) & (position < limit) & (position == wanted) & (late == (lane >= TOK))
    return jnp.where(hit, 1.0, 0.0), late, weight


ROUTING = [
    pltpu.SMEM((EXPERTS,), jnp.int32),
    pltpu.SMEM((EXPERTS,), jnp.int32),
    pltpu.VMEM((2, TOK), jnp.int32),
    pltpu.VMEM((2, TOK), F32),
]


def fetch(sources, targets, sems):
    copies = [pltpu.make_async_copy(s, t, sems.at[i]) for i, (s, t) in enumerate(zip(sources, targets))]
    for copy in copies:
        copy.start()
    return copies


def pack(routing, tokens, grad_out):
    def kernel(*refs):
        sources, outs, (counts, hosted, picks, gates, values, sems) = refs[:6], refs[6:10], refs[10:]
        targets = [counts, hosted, picks, gates, values.at[:TOK], values.at[TOK:]]
        for copy in fetch(sources, targets, sems):
            copy.wait()
        one_hot, late, weight = slots_of(counts, hosted, picks[...], gates[...])
        scale = jnp.sum(jnp.where(late, one_hot * weight, one_hot), axis=1, keepdims=True)
        rows = jnp.dot(one_hot.astype(BF16), values[...], preferred_element_type=F32) * scale
        for m in range(4):
            outs[m][...] = rows[m * PAIR : (m + 1) * PAIR].astype(BF16)

    scratch = ROUTING + [pltpu.VMEM((2 * TOK, WIDTH), BF16), pltpu.SemaphoreType.DMA((6,))]
    shapes = [((PAIR, WIDTH), BF16)] * 4
    return call(kernel, "pack", [HBM] * 6, shapes, (*routing, tokens, grad_out), scratch=scratch)


def combine_matrix(routing):
    def kernel(*refs):
        sources, out, targets, sems = refs[:4], refs[4], refs[5:9], refs[9]
        for copy in fetch(sources, targets, sems):
            copy.wait()
        counts, hosted, picks, gates = targets
        one_hot, late, weight = slots_of(counts, hosted, picks[...], gates[...])
        out[...] = jnp.where(late, one_hot, one_hot * weight)

    scratch = ROUTING + [pltpu.SemaphoreType.DMA((4,))]
    return call(kernel, "combine_matrix", [HBM] * 4, [((4 * PAIR, 2 * TOK), F32)], routing, scratch=scratch)[0]


def join_y(parts):
    total = 4 * PAIR

    def kernel(a, c, d, b, out):
        stacked = jnp.concatenate([p[...].astype(F32) for p in (a, b, c, d)], axis=0).astype(BF16)
        to = lax.broadcasted_iota(jnp.int32, (total, total), 0)
        come = lax.broadcasted_iota(jnp.int32, (total, total), 1)
        half = to // BLOCK
        inner = to - half * BLOCK
        source = inner // SLOTS
        wanted = source * PAIR + half * SLOTS + (inner - source * SLOTS)
        order = jnp.where(come == wanted, 1.0, 0.0).astype(BF16)
        out[...] = jnp.dot(order, stacked, preferred_element_type=F32).astype(BF16)

    return call(kernel, "join_y", [VMEM] * 4, [((total, WIDTH), BF16)], parts)[0]


def load_weights(w_gate, w_up, w_down):
    def kernel(wg, wu, wd, both, down, sems):
        targets = [both.at[:, :UNITS], both.at[:, UNITS:], down]
        for copy in fetch([wg.at[0], wu.at[0], wd.at[0]], targets, sems):
            copy.wait()

    shapes = [((4 * WIDTH, 2 * UNITS), BF16), ((UNITS, 4 * WIDTH), BF16)]
    scratch = [pltpu.SemaphoreType.DMA((3,))]
    return call(kernel, "load_weights", [HBM] * 3, shapes, (w_gate, w_up, w_down), scratch=scratch)


def join_first(parts):
    def kernel(a, c, d, b, x_out, cot_out):
        for m, part in enumerate((a, b, c, d)):
            x_out[m] = part[:BLOCK, :]
            cot_out[m] = part[BLOCK:, :]

    return call(kernel, "join_first", [VMEM] * 4, [((4, BLOCK, WIDTH), BF16)] * 2, parts)


def join_second(parts):
    def kernel(a, c, d, b, out):
        for m, part in enumerate((a, b, c, d)):
            out[m] = part[...]

    return call(kernel, "join_second", [VMEM] * 4, [((4, 4, BLOCK, WIDTH), BF16)], parts)[0]


def place(core, xlm, zm, xhm):
    xm = xhm * 2 + xlm
    return jnp.where(core == 0, zm, xm), jnp.where(core == 0, xm, zm)


def rows_of(core, xlm, pieces):
    blocks = [pieces[place(core, xlm, zm, xhm)] for zm in range(4) for xhm in range(2)]
    return jnp.concatenate(blocks, axis=0)


def scatter_rows(core, xlm, rows, out_ref):
    for zm in range(4):
        for xhm in range(2):
            row = (zm * 2 + xhm) * BLOCK
            out_ref[place(core, xlm, zm, xhm)] = rows[row : row + BLOCK].astype(out_ref.dtype)


def at(shard, fm):
    return pl.ds(pl.multiple_of(jnp.bitwise_xor(shard, fm) * WIDTH, WIDTH), WIDTH)


def forward(cm, pieces, w_both, before):
    def kernel(pieces, w, *refs):
        shard = lax.axis_index("shard")
        total, both_ref = None if before is None else refs[0][...], refs[0 if before is None else 1]
        for xlm in range(2):
            rows = rows_of((shard & 1) ^ cm, xlm, pieces)
            part = jnp.dot(rows, w[at(shard, xlm * 2 + cm), :], preferred_element_type=F32)
            total = part if total is None else total + part
        both_ref[...] = total
        if before is not None:
            gate = both_ref[:, :UNITS]
            refs[2][...] = (gate * jax.nn.sigmoid(gate) * both_ref[:, UNITS:]).astype(BF16)

    shapes = [((ROWS, 2 * UNITS), F32)]
    specs, operands = [VMEM, VMEM], (pieces, w_both)
    if before is not None:
        shapes, specs, operands = shapes + [((ROWS, UNITS), BF16)], specs + [VMEM], operands + (before,)
    return call(kernel, f"forward_{cm}", specs, shapes, operands, 8)


def out_rows(cm, hidden, w_down):
    def kernel(hidden, w, out_ref):
        shard = lax.axis_index("shard")
        for xlm in range(2):
            rows = jnp.dot(hidden[...], w[:, at(shard, xlm * 2 + cm)], preferred_element_type=F32)
            scatter_rows((shard & 1) ^ cm, xlm, rows, out_ref)

    shapes = [((4, 4, BLOCK, WIDTH), BF16)]
    return call(kernel, f"out_rows_{cm}", [VMEM, VMEM], shapes, (hidden, w_down))[0]


def backward_hidden(cm, pieces, w_down, before, both):
    def kernel(pieces, w, *refs):
        shard = lax.axis_index("shard")
        total = None if before is None else refs[0][...]
        for xlm in range(2):
            rows = rows_of((shard & 1) ^ cm, xlm, pieces)
            part = lax.dot_general(rows, w[:, at(shard, xlm * 2 + cm)], NT, preferred_element_type=F32)
            total = part if total is None else total + part
        if before is None:
            refs[0][...] = total
            return
        both_ref, d_ref = refs[1:]
        gate, up = both_ref[:, :UNITS], both_ref[:, UNITS:]
        sigma = jax.nn.sigmoid(gate)
        d_ref[:, :UNITS] = (total * up * (sigma * (1.0 + gate * (1.0 - sigma)))).astype(BF16)
        d_ref[:, UNITS:] = (total * (gate * sigma)).astype(BF16)

    name, specs, operands = f"backward_hidden_{cm}", [VMEM, VMEM], (pieces, w_down)
    if before is None:
        return call(kernel, name, specs, [((ROWS, UNITS), F32)], operands)[0]
    shapes = [((ROWS, 2 * UNITS), BF16)]
    return call(kernel, name, specs + [VMEM] * 2, shapes, operands + (before, both))[0]


def back_rows(cm, d_both, w_both):
    def kernel(d, w, out_ref):
        shard = lax.axis_index("shard")
        for xlm in range(2):
            rows = lax.dot_general(d[...], w[at(shard, xlm * 2 + cm), :], NT, preferred_element_type=F32)
            scatter_rows((shard & 1) ^ cm, xlm, rows, out_ref)

    shapes = [((4, 4, BLOCK, WIDTH), BF16)]
    return call(kernel, f"back_rows_{cm}", [VMEM, VMEM], shapes, (d_both, w_both))[0]


def weight_grads(x_pieces, cot_pieces, d_both, hidden):
    def kernel(x_mine, x_theirs, cot_mine, cot_theirs, d, hidden, gate_out, up_out, down_out, both, down, sems):
        shard = lax.axis_index("shard")
        copies = []
        for fm in range(4):
            side = (shard & 1) ^ (fm % 2)
            if fm >= 2:
                wait_all(copies[fm - 2])
            slot = fm % 2
            rows = rows_of(side, fm // 2, x_theirs if fm % 2 else x_mine)
            both[slot] = lax.dot_general(rows, d[...], TN, preferred_element_type=F32).astype(BF16)
            sources = [both.at[slot, :, :UNITS], both.at[slot, :, UNITS:]]
            targets = [gate_out.at[0, at(shard, fm), :], up_out.at[0, at(shard, fm), :]]
            started = fetch(sources, targets, sems.at[slot])
            rows = rows_of(side, fm // 2, cot_theirs if fm % 2 else cot_mine)
            down[slot] = lax.dot_general(hidden[...], rows, TN, preferred_element_type=F32).astype(BF16)
            last = pltpu.make_async_copy(down.at[slot], down_out.at[0, :, at(shard, fm)], sems.at[slot, 2])
            last.start()
            copies.append(started + [last])
        wait_all(copies[2])
        wait_all(copies[3])

    shapes = [((1, 4 * WIDTH, UNITS), BF16)] * 2 + [((1, UNITS, 4 * WIDTH), BF16)]
    scratch = [
        pltpu.VMEM((2, WIDTH, 2 * UNITS), BF16),
        pltpu.VMEM((2, UNITS, WIDTH), BF16),
        pltpu.SemaphoreType.DMA((2, 3)),
    ]
    operands = (*x_pieces, *cot_pieces, d_both, hidden)
    return call(kernel, "weight_grads", [VMEM] * 6, shapes, operands, 14, scratch, HBM)


def wait_all(copies):
    for copy in copies:
        copy.wait()


def sum_cores(mine, theirs):
    def kernel(a, b, *outs):
        for m in range(4):
            outs[m][...] = (a[m].astype(F32) + b[m].astype(F32)).astype(BF16)

    return call(kernel, "sum_cores", [VMEM] * 2, [((4, BLOCK, WIDTH), BF16)] * 4, (mine, theirs))


def sum_second(pieces):
    def kernel(a, c, d, b, *outs):
        for m in range(4):
            total = (a[m].astype(F32) + b[m].astype(F32)) + (c[m].astype(F32) + d[m].astype(F32))
            outs[m][...] = total.astype(outs[m].dtype)

    shapes = [((BLOCK, WIDTH), F32)] + [((BLOCK, WIDTH), BF16)] * 3
    return call(kernel, "sum_second", [VMEM] * 4, shapes, pieces)


def sum_second_both(blocks, pieces):
    def kernel(*refs):
        (a, b, c, d), outs = refs[4:8], refs[8:]
        for m in range(4):
            total = (a[m].astype(F32) + b[m].astype(F32)) + (c[m].astype(F32) + d[m].astype(F32))
            outs[m][:BLOCK, :] = refs[m][...]
            outs[m][BLOCK:, :] = total.astype(outs[m].dtype)

    shapes = [((2 * BLOCK, WIDTH), F32)] + [((2 * BLOCK, WIDTH), BF16)] * 3
    return call(kernel, "sum_second_both", [VMEM] * 8, shapes, (*blocks, *pieces))


def sum_first(blocks):
    def kernel(a, c, d, b, *outs):
        total = (a[...] + b[...].astype(F32)) + (c[...].astype(F32) + d[...].astype(F32))
        for m in range(4):
            halves = [total[half * BLOCK + m * SLOTS :][:SLOTS] for half in range(2)]
            outs[m][...] = jnp.concatenate(halves, axis=0).astype(outs[m].dtype)

    shapes = [((PAIR, WIDTH), F32)] + [((PAIR, WIDTH), BF16)] * 3
    return call(kernel, "sum_first", [VMEM] * 4, shapes, blocks)


def combine(matrix, parts):
    def kernel(matrix, a, c, d, b, outputs, grads):
        stacked = jnp.concatenate([p[...].astype(F32) for p in (a, b, c, d)], axis=0)
        total = lax.dot_general(
            matrix[...], stacked, TN, precision=lax.Precision.HIGHEST, preferred_element_type=F32
        )
        outputs[...] = total[:TOK].astype(BF16)
        grads[...] = total[TOK:].astype(BF16)

    return call(kernel, "combine", [VMEM] * 5, [((TOK, WIDTH), BF16)] * 2, (matrix, *parts), out=VMEM)


def per_device(tokens, routes, gate_probs, prev_counts, hosts, w_gate, w_up, w_down, grad_out):
    routing = (prev_counts, hosts, routes.T, gate_probs.T)
    tie = lax.optimization_barrier
    payload = exchange(pack(routing, tokens, grad_out), over_y)
    payload, matrix = tie((payload, combine_matrix(routing)))
    x_quarter, cot_quarter = join_first(exchange([join_y(payload)] * 4, over_first))
    x_quarters, (w_both, w_down) = tie(
        (exchange([x_quarter] * 4, over_second), load_weights(w_gate, w_up, w_down))
    )
    x_mine = join_second(x_quarters)
    (part,) = forward(0, x_mine, w_both, None)
    own, first, *late = x_quarters
    part, late = tie((part, late))
    x_theirs = [over_core(x) for x in (own, first, *late)]
    cot_mine = join_second(exchange([cot_quarter] * 4, over_second))
    x_theirs, cot_mine, part = tie((x_theirs, cot_mine, part))
    x_theirs = join_second(x_theirs)
    cot_theirs = over_core(cot_mine)
    gate_up, hidden = forward(1, x_theirs, w_both, part)
    out_theirs = over_core(out_rows(1, hidden, w_down))
    part = backward_hidden(0, cot_mine, w_down, None, None)
    out_mine, cot_theirs = tie((out_rows(0, hidden, w_down), cot_theirs))
    d_both = backward_hidden(1, cot_theirs, w_down, part, gate_up)
    back_theirs = over_core(back_rows(1, d_both, w_both))
    out_pieces = exchange(sum_cores(out_mine, out_theirs), over_second)
    back_pieces = exchange(sum_cores(back_rows(0, d_both, w_both), back_theirs), over_second)
    grads = weight_grads((x_mine, x_theirs), (cot_mine, cot_theirs), d_both, hidden)
    back_pieces, out_pieces, grads = tie((back_pieces, out_pieces, grads))
    blocks = exchange(sum_second_both(sum_second(out_pieces), back_pieces), over_first)
    parts = exchange(sum_first(blocks), over_y)
    outputs, grad_tokens = combine(matrix, parts)
    return outputs, grad_tokens, *grads


def solution(mesh):
    rows, weights = P("expert", "shard"), P("expert", None, "shard")
    down = P("expert", "shard", None)
    small = P("expert", None)
    return jax.shard_map(
        per_device,
        mesh=mesh,
        in_specs=(rows, small, small, P(), P(), weights, weights, down, rows),
        out_specs=(rows, rows, weights, weights, down),
        check_vma=False,
    )
```

```python
import jax
import jax.numpy as jnp
from jax import lax
from jax.experimental import pallas as pl
from jax.experimental.pallas import tpu as pltpu
from jax.sharding import PartitionSpec as P

AXES = ("expert", "shard")
EXPERTS = 4
CAP = 6
SLOTS = 12
PAIR = 2 * SLOTS
TOK = 16
BLOCK = 4 * SLOTS
ROWS = 8 * BLOCK
WIDTH = 1024
UNITS = 384
BF16 = jnp.bfloat16
F32 = jnp.float32
MIB = 1 << 20

VMEM = pl.BlockSpec(memory_space=pltpu.VMEM)
HBM = pl.BlockSpec(memory_space=pltpu.HBM)
NT = (((1,), (1,)), ((), ()))
TN = (((0,), (0,)), ((), ()))


def send(value, flip):
    return lax.ppermute(value, AXES, [(i, flip(i)) for i in range(128)])


def over_core(value):
    return send(value, lambda i: i ^ 1)


def over_y(value, mask):
    return send(value, lambda i: i ^ (mask << 5))


def over_first(value, mask):
    return send(value, lambda i: i ^ (mask << (3 if i & 1 else 1)))


def over_second(value, mask):
    return send(value, lambda i: i ^ (mask << (1 if i & 1 else 3)))


ORDER = (0, 2, 3, 1)


def exchange(values, over):
    return [values[0]] + [over(values[m], m) for m in ORDER[1:]]


def call(kernel, name, specs, shapes, operands, mib=8, scratch=(), out=None):
    spaces = {id(VMEM): pltpu.VMEM, id(HBM): pltpu.HBM}
    operands = [
        pltpu.with_memory_space_constraint(x, spaces[id(spec)]) if id(spec) in spaces else x
        for spec, x in zip(specs, operands)
    ]
    return pl.pallas_call(
        kernel,
        out_shape=[jax.ShapeDtypeStruct(s, d) if out else pltpu.VMEM(s, d) for s, d in shapes],
        in_specs=specs,
        out_specs=[out or VMEM] * len(shapes),
        scratch_shapes=list(scratch),
        compiler_params=pltpu.CompilerParams(vmem_limit_bytes=mib * MIB),
        cost_estimate=pl.CostEstimate(flops=0, bytes_accessed=0, transcendentals=0),
        name=name,
    )(*operands)


def slots_of(counts, hosted, picks, gates):
    shape = (4 * PAIR, 2 * TOK)
    row = lax.broadcasted_iota(jnp.int32, shape, 0)
    lane = lax.broadcasted_iota(jnp.int32, shape, 1)
    mask = row // PAIR
    slot = row - mask * PAIR
    expert = jnp.bitwise_xor(mask, lax.axis_index("expert") // 8)
    a = lax.broadcasted_iota(jnp.int32, (2 * TOK, 2 * TOK), 0)
    b = lax.broadcasted_iota(jnp.int32, (2 * TOK, 2 * TOK), 1)
    earlier = jnp.where((a // TOK == b // TOK) & (a < b), 1.0, 0.0)
    late = slot >= SLOTS
    wanted = jnp.where(late, slot - SLOTS, slot)
    picked = jnp.concatenate([picks, picks], axis=1)
    probs = jnp.concatenate([gates, gates], axis=1)
    first = picked[0:1] == expert
    second = picked[1:2] == expert
    has = jnp.where(first | second, 1.0, 0.0)
    weight = jnp.where(first, probs[0:1], 0.0) + jnp.where(second, probs[1:2], 0.0)
    position = jnp.dot(has.astype(BF16), earlier.astype(BF16), preferred_element_type=F32)
    position = position.astype(jnp.int32)
    limit = jnp.zeros(shape, jnp.int32)
    for e in range(EXPERTS):
        quota = jnp.minimum((counts[e] + 63) // 64, CAP)
        limit = jnp.where(expert == e, quota + hosted[e ^ 1], limit)
    hit = (has > 0.5) & (position < limit) & (position == wanted) & (late == (lane >= TOK))
    return jnp.where(hit, 1.0, 0.0), late, weight


ROUTING = [
    pltpu.SMEM((EXPERTS,), jnp.int32),
    pltpu.SMEM((EXPERTS,), jnp.int32),
    pltpu.VMEM((2, TOK), jnp.int32),
    pltpu.VMEM((2, TOK), F32),
]


def fetch(sources, targets, sems):
    copies = [pltpu.make_async_copy(s, t, sems.at[i]) for i, (s, t) in enumerate(zip(sources, targets))]
    for copy in copies:
        copy.start()
    return copies


def pack(routing, tokens, grad_out):
    def kernel(*refs):
        sources, outs, (counts, hosted, picks, gates, values, sems) = refs[:6], refs[6:10], refs[10:]
        targets = [counts, hosted, picks, gates, values.at[:TOK], values.at[TOK:]]
        copies = fetch(sources, targets, sems)
        wait_all(copies[:4])
        one_hot, late, weight = slots_of(counts, hosted, picks[...], gates[...])
        scale = jnp.sum(jnp.where(late, one_hot * weight, one_hot), axis=1, keepdims=True)
        wait_all(copies[4:])
        rows = jnp.dot(one_hot.astype(BF16), values[...], preferred_element_type=F32) * scale
        for m in range(4):
            outs[m][...] = rows[m * PAIR : (m + 1) * PAIR].astype(BF16)

    scratch = ROUTING + [pltpu.VMEM((2 * TOK, WIDTH), BF16), pltpu.SemaphoreType.DMA((6,))]
    shapes = [((PAIR, WIDTH), BF16)] * 4
    return call(kernel, "pack", [HBM] * 6, shapes, (*routing, tokens, grad_out), scratch=scratch)


def combine_matrix(routing):
    def kernel(*refs):
        sources, out, targets, sems = refs[:4], refs[4], refs[5:9], refs[9]
        for copy in fetch(sources, targets, sems):
            copy.wait()
        counts, hosted, picks, gates = targets
        one_hot, late, weight = slots_of(counts, hosted, picks[...], gates[...])
        out[...] = jnp.where(late, one_hot, one_hot * weight)

    scratch = ROUTING + [pltpu.SemaphoreType.DMA((4,))]
    return call(kernel, "combine_matrix", [HBM] * 4, [((4 * PAIR, 2 * TOK), F32)], routing, scratch=scratch)[0]


def join_y(parts):
    total = 4 * PAIR

    def kernel(a, c, d, b, out):
        stacked = jnp.concatenate([p[...].astype(F32) for p in (a, b, c, d)], axis=0).astype(BF16)
        to = lax.broadcasted_iota(jnp.int32, (total, total), 0)
        come = lax.broadcasted_iota(jnp.int32, (total, total), 1)
        half = to // BLOCK
        inner = to - half * BLOCK
        source = inner // SLOTS
        wanted = source * PAIR + half * SLOTS + (inner - source * SLOTS)
        order = jnp.where(come == wanted, 1.0, 0.0).astype(BF16)
        out[...] = jnp.dot(order, stacked, preferred_element_type=F32).astype(BF16)

    return call(kernel, "join_y", [VMEM] * 4, [((total, WIDTH), BF16)], parts)[0]


def load_weights(w_gate, w_up, w_down):
    def kernel(wg, wu, wd, both, down, sems):
        targets = [both.at[:, :UNITS], both.at[:, UNITS:], down]
        for copy in fetch([wg.at[0], wu.at[0], wd.at[0]], targets, sems):
            copy.wait()

    shapes = [((4 * WIDTH, 2 * UNITS), BF16), ((UNITS, 4 * WIDTH), BF16)]
    scratch = [pltpu.SemaphoreType.DMA((3,))]
    return call(kernel, "load_weights", [HBM] * 3, shapes, (w_gate, w_up, w_down), scratch=scratch)


def join_first(parts):
    def kernel(a, c, d, b, x_out, cot_out):
        for m, part in enumerate((a, b, c, d)):
            x_out[m] = part[:BLOCK, :]
            cot_out[m] = part[BLOCK:, :]

    return call(kernel, "join_first", [VMEM] * 4, [((4, BLOCK, WIDTH), BF16)] * 2, parts)


def join_second(parts):
    def kernel(a, c, d, b, out):
        for m, part in enumerate((a, b, c, d)):
            out[m] = part[...]

    return call(kernel, "join_second", [VMEM] * 4, [((4, 4, BLOCK, WIDTH), BF16)], parts)[0]


def place(core, xlm, zm, xhm):
    xm = xhm * 2 + xlm
    return jnp.where(core == 0, zm, xm), jnp.where(core == 0, xm, zm)


def rows_of(core, xlm, pieces):
    blocks = [pieces[place(core, xlm, zm, xhm)] for zm in range(4) for xhm in range(2)]
    return jnp.concatenate(blocks, axis=0)


def scatter_rows(core, xlm, rows, out_ref):
    for zm in range(4):
        for xhm in range(2):
            row = (zm * 2 + xhm) * BLOCK
            out_ref[place(core, xlm, zm, xhm)] = rows[row : row + BLOCK].astype(out_ref.dtype)


def at(shard, fm):
    return pl.ds(pl.multiple_of(jnp.bitwise_xor(shard, fm) * WIDTH, WIDTH), WIDTH)


def forward(cm, pieces, w_both, before):
    def kernel(pieces, w, *refs):
        shard = lax.axis_index("shard")
        total, both_ref = None if before is None else refs[0][...], refs[0 if before is None else 1]
        for xlm in range(2):
            rows = rows_of((shard & 1) ^ cm, xlm, pieces)
            part = jnp.dot(rows, w[at(shard, xlm * 2 + cm), :], preferred_element_type=F32)
            total = part if total is None else total + part
        both_ref[...] = total
        if before is not None:
            gate = both_ref[:, :UNITS]
            refs[2][...] = (gate * jax.nn.sigmoid(gate) * both_ref[:, UNITS:]).astype(BF16)

    shapes = [((ROWS, 2 * UNITS), F32)]
    specs, operands = [VMEM, VMEM], (pieces, w_both)
    if before is not None:
        shapes, specs, operands = shapes + [((ROWS, UNITS), BF16)], specs + [VMEM], operands + (before,)
    return call(kernel, f"forward_{cm}", specs, shapes, operands, 8)


def out_rows(cm, hidden, w_down):
    def kernel(hidden, w, out_ref):
        shard = lax.axis_index("shard")
        for xlm in range(2):
            rows = jnp.dot(hidden[...], w[:, at(shard, xlm * 2 + cm)], preferred_element_type=F32)
            scatter_rows((shard & 1) ^ cm, xlm, rows, out_ref)

    shapes = [((4, 4, BLOCK, WIDTH), BF16)]
    return call(kernel, f"out_rows_{cm}", [VMEM, VMEM], shapes, (hidden, w_down))[0]


def backward_hidden(cm, pieces, w_down, before, both):
    def kernel(pieces, w, *refs):
        shard = lax.axis_index("shard")
        total = None if before is None else refs[0][...]
        for xlm in range(2):
            rows = rows_of((shard & 1) ^ cm, xlm, pieces)
            part = lax.dot_general(rows, w[:, at(shard, xlm * 2 + cm)], NT, preferred_element_type=F32)
            total = part if total is None else total + part
        if before is None:
            refs[0][...] = total
            return
        both_ref, d_ref = refs[1:]
        gate, up = both_ref[:, :UNITS], both_ref[:, UNITS:]
        sigma = jax.nn.sigmoid(gate)
        d_ref[:, :UNITS] = (total * up * (sigma * (1.0 + gate * (1.0 - sigma)))).astype(BF16)
        d_ref[:, UNITS:] = (total * (gate * sigma)).astype(BF16)

    name, specs, operands = f"backward_hidden_{cm}", [VMEM, VMEM], (pieces, w_down)
    if before is None:
        return call(kernel, name, specs, [((ROWS, UNITS), F32)], operands)[0]
    shapes = [((ROWS, 2 * UNITS), BF16)]
    return call(kernel, name, specs + [VMEM] * 2, shapes, operands + (before, both))[0]


def back_rows(cm, d_both, w_both):
    def kernel(d, w, out_ref):
        shard = lax.axis_index("shard")
        for xlm in range(2):
            rows = lax.dot_general(d[...], w[at(shard, xlm * 2 + cm), :], NT, preferred_element_type=F32)
            scatter_rows((shard & 1) ^ cm, xlm, rows, out_ref)

    shapes = [((4, 4, BLOCK, WIDTH), BF16)]
    return call(kernel, f"back_rows_{cm}", [VMEM, VMEM], shapes, (d_both, w_both))[0]


def weight_grads(x_pieces, cot_pieces, d_both, hidden):
    def kernel(x_mine, x_theirs, cot_mine, cot_theirs, d, hidden, gate_out, up_out, down_out, both, down, sems):
        shard = lax.axis_index("shard")
        copies = []
        for fm in range(4):
            side = (shard & 1) ^ (fm % 2)
            if fm >= 2:
                wait_all(copies[fm - 2])
            slot = fm % 2
            rows = rows_of(side, fm // 2, x_theirs if fm % 2 else x_mine)
            both[slot] = lax.dot_general(rows, d[...], TN, preferred_element_type=F32).astype(BF16)
            sources = [both.at[slot, :, :UNITS], both.at[slot, :, UNITS:]]
            targets = [gate_out.at[0, at(shard, fm), :], up_out.at[0, at(shard, fm), :]]
            started = fetch(sources, targets, sems.at[slot])
            rows = rows_of(side, fm // 2, cot_theirs if fm % 2 else cot_mine)
            down[slot] = lax.dot_general(hidden[...], rows, TN, preferred_element_type=F32).astype(BF16)
            last = pltpu.make_async_copy(down.at[slot], down_out.at[0, :, at(shard, fm)], sems.at[slot, 2])
            last.start()
            copies.append(started + [last])
        wait_all(copies[2])
        wait_all(copies[3])

    shapes = [((1, 4 * WIDTH, UNITS), BF16)] * 2 + [((1, UNITS, 4 * WIDTH), BF16)]
    scratch = [
        pltpu.VMEM((2, WIDTH, 2 * UNITS), BF16),
        pltpu.VMEM((2, UNITS, WIDTH), BF16),
        pltpu.SemaphoreType.DMA((2, 3)),
    ]
    operands = (*x_pieces, *cot_pieces, d_both, hidden)
    return call(kernel, "weight_grads", [VMEM] * 6, shapes, operands, 14, scratch, HBM)


def wait_all(copies):
    for copy in copies:
        copy.wait()


def sum_cores(mine, theirs):
    def kernel(a, b, *outs):
        for m in range(4):
            outs[m][...] = (a[m].astype(F32) + b[m].astype(F32)).astype(BF16)

    return call(kernel, "sum_cores", [VMEM] * 2, [((4, BLOCK, WIDTH), BF16)] * 4, (mine, theirs))


def sum_second(pieces):
    def kernel(a, c, d, b, *outs):
        for m in range(4):
            total = (a[m].astype(F32) + b[m].astype(F32)) + (c[m].astype(F32) + d[m].astype(F32))
            outs[m][...] = total.astype(outs[m].dtype)

    shapes = [((BLOCK, WIDTH), F32)] + [((BLOCK, WIDTH), BF16)] * 3
    return call(kernel, "sum_second", [VMEM] * 4, shapes, pieces)


def sum_second_both(blocks, pieces):
    def kernel(*refs):
        (a, b, c, d), outs = refs[4:8], refs[8:]
        for m in range(4):
            total = (a[m].astype(F32) + b[m].astype(F32)) + (c[m].astype(F32) + d[m].astype(F32))
            outs[m][:BLOCK, :] = refs[m][...]
            outs[m][BLOCK:, :] = total.astype(outs[m].dtype)

    shapes = [((2 * BLOCK, WIDTH), F32)] + [((2 * BLOCK, WIDTH), BF16)] * 3
    return call(kernel, "sum_second_both", [VMEM] * 8, shapes, (*blocks, *pieces))


def sum_first(blocks):
    def kernel(a, c, d, b, *outs):
        total = (a[...] + b[...].astype(F32)) + (c[...].astype(F32) + d[...].astype(F32))
        for m in range(4):
            halves = [total[half * BLOCK + m * SLOTS :][:SLOTS] for half in range(2)]
            outs[m][...] = jnp.concatenate(halves, axis=0).astype(outs[m].dtype)

    shapes = [((PAIR, WIDTH), F32)] + [((PAIR, WIDTH), BF16)] * 3
    return call(kernel, "sum_first", [VMEM] * 4, shapes, blocks)


def combine(matrix, parts):
    def kernel(matrix, a, c, d, b, outputs, grads):
        stacked = jnp.concatenate([p[...].astype(F32) for p in (a, b, c, d)], axis=0)
        total = lax.dot_general(
            matrix[...], stacked, TN, precision=lax.Precision.HIGHEST, preferred_element_type=F32
        )
        outputs[...] = total[:TOK].astype(BF16)
        grads[...] = total[TOK:].astype(BF16)

    return call(kernel, "combine", [VMEM] * 5, [((TOK, WIDTH), BF16)] * 2, (matrix, *parts), out=VMEM)


def per_device(tokens, routes, gate_probs, prev_counts, hosts, w_gate, w_up, w_down, grad_out):
    routing = (prev_counts, hosts, routes.T, gate_probs.T)
    tie = lax.optimization_barrier
    payload = exchange(pack(routing, tokens, grad_out), over_y)
    payload, matrix = tie((payload, combine_matrix(routing)))
    x_quarter, cot_quarter = join_first(exchange([join_y(payload)] * 4, over_first))
    x_quarters, (w_both, w_down) = tie(
        (exchange([x_quarter] * 4, over_second), load_weights(w_gate, w_up, w_down))
    )
    x_mine = join_second(x_quarters)
    (part,) = forward(0, x_mine, w_both, None)
    own, first, *late = x_quarters
    part, late = tie((part, late))
    x_theirs = [over_core(x) for x in (own, first, *late)]
    cot_mine = join_second(exchange([cot_quarter] * 4, over_second))
    x_theirs, cot_mine, part = tie((x_theirs, cot_mine, part))
    x_theirs = join_second(x_theirs)
    cot_theirs = over_core(cot_mine)
    gate_up, hidden = forward(1, x_theirs, w_both, part)
    out_theirs = over_core(out_rows(1, hidden, w_down))
    part = backward_hidden(0, cot_mine, w_down, None, None)
    out_mine = out_rows(0, hidden, w_down)
    d_both = backward_hidden(1, cot_theirs, w_down, part, gate_up)
    back_theirs = over_core(back_rows(1, d_both, w_both))
    out_pieces = exchange(sum_cores(out_mine, out_theirs), over_second)
    back_pieces = exchange(sum_cores(back_rows(0, d_both, w_both), back_theirs), over_second)
    grads = weight_grads((x_mine, x_theirs), (cot_mine, cot_theirs), d_both, hidden)
    back_pieces, out_pieces, grads = tie((back_pieces, out_pieces, grads))
    blocks = exchange(sum_second_both(sum_second(out_pieces), back_pieces), over_first)
    parts = exchange(sum_first(blocks), over_y)
    outputs, grad_tokens = combine(matrix, parts)
    return outputs, grad_tokens, *grads


def solution(mesh):
    rows, weights = P("expert", "shard"), P("expert", None, "shard")
    down = P("expert", "shard", None)
    small = P("expert", None)
    return jax.shard_map(
        per_device,
        mesh=mesh,
        in_specs=(rows, small, small, P(), P(), weights, weights, down, rows),
        out_specs=(rows, rows, weights, weights, down),
        check_vma=False,
    )
```
